32 devices in a mesh: seq: 8 (over z, y), head: 4 (over x, core).
Axes of the slice: x: 2, y: 2, z: 4, core: 2. Of those that a mesh axis runs over, the one named last changes fastest.
Arguments:
- x_in: bfloat16 [4096, 8192], P('seq', 'head'), may hold values from -6 to 6
- bc_in: bfloat16 [4096, 4, 256], P('seq', 'head'), may hold values from -6 to 6
- z_in: bfloat16 [4096, 8192], P('seq', 'head'), may hold values from -6 to 6
- dt_raw: bfloat16 [128, 4096], P('head', 'seq'), may hold values from -20 to 4
- a_log: float32 [128], P('head'), may hold values from -6 to 0.7
- conv_x: float32 [4, 8192], P(None, 'head'), may hold values from -3 to 3
- conv_bc: float32 [4, 4, 256], P(None, 'head'), may hold values from -3 to 3
- d_skip: float32 [128], P('head'), may hold values from 0.5 to 2
- norm_gain: float32 [8192], P('head'), may hold values from 0.25 to 1.75
- out_weight: bfloat16 [8192, 4096], P('head'), may hold values from -0.09375 to 0.09375
Outputs:
- out: bfloat16 [4096, 4096], P('head', 'seq')
The draws below stay inside these ranges and needn't reach their ends.
All inputs are finite; a program needn't handle non-finite values.
Results may differ from the reference program's by a relative error of at most 0.02.
Values may be sent and summed in bfloat16 or wider, within the bound.
A program may use at most 192 MiB of HBM per device.

```python
import math
import jax
import jax.numpy as jnp
from jax import lax

HEAD_TOTAL = 128
HEAD_DIM = 64
STATE = 128
GROUPS = 4
D_OUT = 4096
CONV = 4
SPAN = 128
INNER = 8192
TOKEN_TOTAL = 4096
N_HEAD = 4


def decay_tables(key):
    base_key = jax.random.fold_in(key, 4242)
    random_keys = jax.random.split(base_key, 9)
    fast_heads = jax.random.randint(random_keys[0], (HEAD_TOTAL,), 0, 2) == 0
    fast_scale = jnp.exp(jax.random.uniform(random_keys[1], (HEAD_TOTAL,), jnp.float32, -0.7, 0.7))
    fast_rate = jnp.exp(jax.random.uniform(random_keys[2], (HEAD_TOTAL,), jnp.float32, math.log(1.0 / 50.0), math.log(1.0 / 30.0)))
    slow_total = jnp.exp(jax.random.uniform(random_keys[3], (HEAD_TOTAL,), jnp.float32, math.log(0.6), math.log(1.2)))
    slow_level = 2.5 / math.sqrt(STATE * TOKEN_TOTAL) * jnp.exp(jax.random.uniform(random_keys[8], (HEAD_TOTAL,), jnp.float32, -0.3, 0.3))
    slow_scale = slow_total / (TOKEN_TOTAL * slow_level * 1.151)
    decay_absolute = jnp.where(fast_heads, fast_scale, slow_scale)
    level_step = jnp.where(fast_heads, fast_rate / fast_scale, slow_level)
    rough_factor = jnp.exp(0.35 * jax.random.truncated_normal(random_keys[4], -2.5, 2.5, (HEAD_TOTAL, TOKEN_TOTAL), jnp.float32))
    block_len = max(TOKEN_TOTAL // 32, 1)
    block_count = TOKEN_TOTAL // block_len
    block_factor = jnp.exp(jax.random.uniform(random_keys[5], (HEAD_TOTAL, block_count), jnp.float32, -0.7, 0.7))
    block_factor = jnp.repeat(block_factor, block_len, axis=1)
    update_rounds = level_step[:, None] * rough_factor * block_factor
    segment_width = min(16, max(TOKEN_TOTAL // 8, 1))
    segment_offsets = jax.random.randint(random_keys[6], (HEAD_TOTAL, 2), 0, TOKEN_TOTAL - segment_width + 1)
    segment_error = -jnp.log(1.0 - jax.random.uniform(random_keys[7], (HEAD_TOTAL, 2), jnp.float32, 0.2, 0.3))
    segment_stride = segment_error / (decay_absolute[:, None] * segment_width)
    token_places = jnp.arange(TOKEN_TOTAL)[None, :]
    for segment_index in range(2):
        leading_token = segment_offsets[:, segment_index:segment_index + 1]
        within_segment = (token_places >= leading_token) & (token_places < leading_token + segment_width)
        update_rounds = jnp.where(within_segment, segment_stride[:, segment_index:segment_index + 1], update_rounds)
    return (decay_absolute, update_rounds)


def draw_dt_raw(key, part):
    decay_absolute, update_rounds = decay_tables(key)
    logits = update_rounds + jnp.log(-jnp.expm1(-update_rounds))
    return logits.astype(jnp.bfloat16)


def draw_a_log(key, part):
    decay_absolute, update_rounds = decay_tables(key)
    return jnp.log(decay_absolute).astype(jnp.float32)


def strengthened(array, stream_key, source, target, shards_of, factor):
    owner, partner = [(jnp.arange(array.shape[position]) // (array.shape[position] // shards_of)).reshape([-1 if axis == position else 1 for axis in range(array.ndim)]) for position in (source, target)]
    chosen = jax.random.permutation(stream_key, shards_of)[partner]
    strong = (owner == chosen) | (owner == (partner + shards_of // 2) % shards_of)
    return jnp.where(strong, factor * array, array)


def shard_levels(key, extent, cuts, smallest, top_value):
    level = 1.0
    for position, shards_of in cuts:
        heights = jax.random.uniform(jax.random.fold_in(jax.random.fold_in(key, 6), position), (shards_of,), jnp.float32, smallest / len(cuts), top_value / len(cuts))
        level = level * jnp.repeat(jnp.exp(heights), extent[position] // shards_of).reshape((-1,) + (1,) * (len(extent) - 1 - position))
    return level


def gaussian(rng, shape, width, bound, cuts=(), held_as=jnp.bfloat16):
    level = shard_levels(rng, shape, cuts, -0.22, 0.18) if cuts else 1.0
    values = jax.random.normal(rng, shape, jnp.float32) * width * level
    return jnp.minimum(jnp.maximum(values, -bound), bound).astype(held_as)


def noise_with(own_key, shape, deviation, reach, pieces, heavy, kind=jnp.bfloat16):
    values = deviation * jax.random.normal(own_key, shape, jnp.float32)
    if pieces:
        values = values * shard_levels(own_key, shape, pieces, -0.22, 0.18)
    return jnp.clip(strengthened(values, jax.random.fold_in(own_key, 3), *heavy), -reach, reach).astype(kind)


def setup_inputs(seed: int = 0) -> dict:
    key_list = jax.random.split(jax.random.key(seed), 11)
    x_in = gaussian(key_list[0], (TOKEN_TOTAL, INNER), 1.0, 6.0, ((0, 8), (1, 4)))
    bc_in = gaussian(key_list[1], (TOKEN_TOTAL, GROUPS, 2 * STATE), 1.0, 6.0, ((0, 8), (1, 4)))
    z_in = gaussian(key_list[2], (TOKEN_TOTAL, INNER), 1.0, 6.0, ((0, 8), (1, 4)))
    dt_raw = draw_dt_raw(jax.random.fold_in(key_list[10], 71), 0)
    a_log = draw_a_log(jax.random.fold_in(key_list[10], 71), 0)
    conv_x = gaussian(key_list[5], (CONV, INNER), CONV ** -0.5, 3.0, ((1, 4),), jnp.float32)
    conv_bc = gaussian(key_list[6], (CONV, GROUPS, 2 * STATE), CONV ** -0.5, 3.0, ((1, 4),), jnp.float32)
    d_skip = jnp.clip(0.5 + 1.5 * jax.random.uniform(key_list[7], (HEAD_TOTAL,), jnp.float32) ** shard_levels(key_list[7], (HEAD_TOTAL,), ((0, 4),), -0.2, 0.2), 0.5, 2.0)
    norm_gain = jnp.clip(1.0 + 0.15 * jax.random.normal(key_list[8], (INNER,), jnp.float32), 0.25, 1.75)
    out_weight = noise_with(key_list[9], (INNER, D_OUT), INNER ** -0.5, 0.09375, ((0, 4),), (0, 1, 4, 2.0))
    return {"x_in": x_in, "bc_in": bc_in, "z_in": z_in, "dt_raw": dt_raw, "a_log": a_log, "conv_x": conv_x, "conv_bc": conv_bc, "d_skip": d_skip, "norm_gain": norm_gain, "out_weight": out_weight}


def conv_silu(extended, weight, rows):
    running = weight[0] * extended[0:rows].astype(jnp.float32)
    for offset in range(1, weight.shape[0]):
        running = running + weight[offset] * extended[offset:offset + rows].astype(jnp.float32)
    return (running * jax.nn.sigmoid(running)).astype(jnp.bfloat16)

def reference(x_in, bc_in, z_in, dt_raw, a_log, conv_x, conv_bc, d_skip, norm_gain, out_weight):
    heads_group = HEAD_TOTAL // GROUPS
    blocks = TOKEN_TOTAL // SPAN
    x_conv = conv_silu(jnp.concatenate([jnp.zeros((CONV - 1, INNER), jnp.bfloat16), x_in], 0), conv_x, TOKEN_TOTAL)
    bc_conv = conv_silu(jnp.concatenate([jnp.zeros((CONV - 1, GROUPS, 2 * STATE), jnp.bfloat16), bc_in], 0), conv_bc, TOKEN_TOTAL)
    b_blocks = bc_conv[:, :, :STATE].reshape(blocks, SPAN, GROUPS, STATE)
    c_blocks = bc_conv[:, :, STATE:].reshape(blocks, SPAN, GROUPS, STATE)
    x_blocks = x_conv.reshape(blocks, SPAN, GROUPS, heads_group, HEAD_DIM)
    z_blocks = z_in.reshape(blocks, SPAN, INNER)
    step_size = jax.nn.softplus(dt_raw.astype(jnp.float32))
    rate = -jnp.exp(a_log)[:, None] * step_size
    step_blocks = jnp.transpose(step_size.reshape(GROUPS, heads_group, blocks, SPAN), (2, 0, 1, 3))
    rate_blocks = jnp.transpose(rate.reshape(GROUPS, heads_group, blocks, SPAN), (2, 0, 1, 3))
    weight_full = out_weight.astype(jnp.float32).reshape(N_HEAD, INNER // N_HEAD, D_OUT)
    row_ids = lax.broadcasted_iota(jnp.int32, (SPAN, SPAN), 0)
    col_ids = lax.broadcasted_iota(jnp.int32, (SPAN, SPAN), 1)
    causal = row_ids >= col_ids
    skip_table = d_skip.reshape(GROUPS, heads_group, 1)

    def one_block(state, inputs):
        x_blk, b_blk, c_blk, step_blk, rate_blk, z_blk = inputs
        log_decay = jnp.cumsum(rate_blk, axis=2)
        scores = jnp.einsum('tgn,sgn->gts', c_blk.astype(jnp.float32), b_blk.astype(jnp.float32))
        decay_gap = log_decay[..., :, None] - log_decay[..., None, :]
        mask_decay = jnp.where(causal, jnp.exp(jnp.where(causal, decay_gap, 0.0)), 0.0)
        mixing = (scores[:, None] * mask_decay * step_blk[..., None, :]).astype(jnp.bfloat16)
        y_intra = jnp.einsum('ghts,sghp->tghp', mixing.astype(jnp.float32), x_blk.astype(jnp.float32))
        tail_weight = jnp.exp(log_decay[..., -1:] - log_decay) * step_blk
        weighted_b = (tail_weight[..., None] * jnp.transpose(b_blk, (1, 0, 2))[:, None].astype(jnp.float32)).astype(jnp.bfloat16)
        block_state = jnp.einsum('sghp,ghsn->ghpn', x_blk.astype(jnp.float32), weighted_b.astype(jnp.float32))
        readout = jnp.einsum('tgn,ghpn->ghtp', c_blk.astype(jnp.float32), state, precision=lax.Precision.HIGHEST)
        y_state = jnp.exp(log_decay)[..., None] * readout
        summed = y_intra + jnp.transpose(y_state, (2, 0, 1, 3)) + skip_table * x_blk.astype(jnp.float32)
        gated_rows = summed.reshape(SPAN, INNER) * jax.nn.silu(z_blk.astype(jnp.float32))
        grouped = gated_rows.reshape(SPAN, GROUPS, INNER // GROUPS)
        inverse_rms = lax.rsqrt(lax.optimization_barrier(jnp.mean(grouped * grouped, axis=2, keepdims=True)) + 1e-05)
        normed = ((grouped * inverse_rms).reshape(SPAN, INNER) * norm_gain).astype(jnp.bfloat16)
        partial_terms = jnp.einsum('tkc,kcd->ktd', normed.astype(jnp.float32).reshape(SPAN, N_HEAD, INNER // N_HEAD), weight_full)
        rounded = lax.optimization_barrier(partial_terms.astype(jnp.bfloat16))
        result = lax.optimization_barrier(jnp.sum(rounded.astype(jnp.float32), axis=0)).astype(jnp.bfloat16)
        new_state = jnp.exp(log_decay[..., -1])[..., None, None] * state + block_state
        return (new_state, result)
    start_state = jnp.zeros((GROUPS, heads_group, HEAD_DIM, STATE), jnp.float32)
    final_state, outputs = lax.scan(one_block, start_state, (x_blocks, b_blocks, c_blocks, step_blocks, rate_blocks, z_blocks))
    return outputs.reshape(TOKEN_TOTAL, D_OUT).T
```

```python
import functools

import jax
import jax.numpy as jnp
from jax import lax
from jax.experimental import pallas as pl
from jax.experimental.pallas import tpu as pltpu
from jax.sharding import PartitionSpec as P

SPAN = 128
MESH = pl.DeviceIdType.MESH
F32 = jnp.float32
BF16 = jnp.bfloat16
LANES = 512
RIM = 16


def half_tanh_silu(u):
    return 0.5 * u * (1.0 + jnp.tanh(0.5 * u))


def conv_silu(before, now, taps):
    cat = jnp.concatenate([before.astype(F32), now.astype(F32)], 0)
    width = taps.shape[0]
    total = taps[width - 1 : width] * cat[RIM:]
    for k in range(width - 1):
        total = total + taps[k : k + 1] * pltpu.roll(cat, width - 1 - k, 0)[RIM:]
    return half_tanh_silu(total)


def split_two(value):
    high = value.astype(BF16)
    low = (value - high.astype(F32)).astype(BF16)
    return jnp.concatenate([high, low], 1)


def scan_kernel(
    n_seq, x_ref, bc_ref, z_ref, dt_ref, alog_ref, cx_ref, cbc_ref, skip_ref, gain_ref, out_ref,
    halo_x, halo_bc, xconv, b_t, c_mat, score, ld_row, st_row, ld_col, t_split, pick_tail, pick_exp,
    decay_in, decay_blk, decay_own, decay_other, skip_row, local_in, final, y_ref, enter,
    y_send, y_recv, z_send, z_recv,
    halo_sems, dec_sems, ys_sem, yr_sem, zs_sem, zr_sem,
):
    tokens, inner = x_ref.shape
    heads = dt_ref.shape[0]
    state = b_t.shape[1]
    width = inner // heads
    blocks = tokens // SPAN
    chunks = inner // LANES
    per = heads // chunks
    rows = n_seq // 2
    q = lax.axis_index("seq")
    odd = lax.rem(q, 2)
    place = q // 2
    pair = q + 1 - 2 * odd
    after = lax.rem(q + 1, n_seq)
    ahead = lax.rem(q + 2, n_seq)

    barrier = pltpu.get_barrier_semaphore()
    pl.semaphore_signal(barrier, inc=1, device_id={"seq": pair}, device_id_type=MESH)

    @pl.when(q > 0)
    def _():
        pl.semaphore_signal(barrier, inc=1, device_id={"seq": q - 1}, device_id_type=MESH)

    @pl.when(q > 1)
    def _():
        pl.semaphore_signal(barrier, inc=1, device_id={"seq": q - 2}, device_id_type=MESH)

    peers = 1 + jnp.minimum(n_seq - 1 - q, 1) + jnp.minimum(jnp.maximum(n_seq - 2 - q, 0), 1)
    pl.semaphore_wait(barrier, peers)

    def send(src, dst, s, r, to):
        return pltpu.make_async_remote_copy(
            src_ref=src, dst_ref=dst, send_sem=s, recv_sem=r, device_id={"seq": to}, device_id_type=MESH
        )

    halo_copies = [
        send(x_ref.at[pl.ds(tokens - RIM, RIM)], halo_x, halo_sems.at[0], halo_sems.at[1], after),
        send(bc_ref.at[pl.ds(tokens - RIM, RIM)], halo_bc, halo_sems.at[2], halo_sems.at[3], after),
    ]

    @pl.when(q < n_seq - 1)
    def _():
        for copy in halo_copies:
            copy.start()

    r_id = lax.broadcasted_iota(jnp.int32, (SPAN, SPAN), 0)
    c_id = lax.broadcasted_iota(jnp.int32, (SPAN, SPAN), 1)
    upto = jnp.where(r_id <= c_id, 1.0, 0.0).astype(F32)
    hr = lax.broadcasted_iota(jnp.int32, (heads, heads), 0)
    hc = lax.broadcasted_iota(jnp.int32, (heads, heads), 1)
    neg_a = -jnp.sum(jnp.where(hr == hc, jnp.exp(alog_ref[...]), 0.0), axis=1, keepdims=True)
    p_row = lax.rem(lax.broadcasted_iota(jnp.int32, (2 * SPAN, inner), 0), SPAN)
    p_head = lax.broadcasted_iota(jnp.int32, (2 * SPAN, inner), 1) // width
    pick_tail[...] = jnp.where(p_row == heads + p_head, 1.0, 0.0).astype(BF16)
    pick_exp[...] = jnp.where(p_row == 2 * heads + p_head, 1.0, 0.0).astype(BF16)
    skip_pad = jnp.concatenate(
        [jnp.zeros((8, 2 * heads), F32), jnp.broadcast_to(skip_ref[...], (8, heads)), jnp.zeros((8, heads), F32)], 1
    )
    skip_row[...] = jnp.dot(split_two(skip_pad), pick_exp[...], preferred_element_type=F32)
    running = jnp.ones((8, inner), F32)
    for b in range(blocks):
        dt = dt_ref[:, b * SPAN : (b + 1) * SPAN].astype(F32)
        e = jnp.exp(-jnp.abs(dt))
        log1p = jnp.where(e < 0.01, e * (1.0 - e * (0.5 - e * (1.0 / 3.0 - 0.25 * e))), jnp.log(1.0 + e))
        step = jnp.maximum(dt, 0.0) + log1p
        ld = jnp.dot(neg_a * step, upto, preferred_element_type=F32, precision=lax.Precision.HIGHEST)
        tail = jnp.exp(ld[:, SPAN - 1 : SPAN] - ld) * step
        table = jnp.concatenate([ld, tail, jnp.exp(ld), step], 0)
        if 4 * heads < SPAN:
            table = jnp.concatenate([table, jnp.zeros((SPAN - 4 * heads, SPAN), F32)], 0)
        turned = table.T
        ld_row[b] = ld
        st_row[b] = step
        for c in range(chunks):
            ld_col[b, c] = turned[:, c * per : (c + 1) * per]
        both = split_two(turned)
        t_split[b] = both
        last = jnp.dot(both[SPAN - 16 :], pick_exp[...], preferred_element_type=F32)[15:16]
        decay_in[b] = running
        decay_blk[b] = jnp.broadcast_to(last, (8, inner))
        running = running * last
    decay_own[...] = running
    dec_copy = send(decay_own, decay_other, dec_sems.at[0], dec_sems.at[1], pair)
    dec_copy.start()

    @pl.when(q > 0)
    def _():
        for copy in halo_copies:
            copy.wait_recv()

    @pl.when(q == 0)
    def _():
        halo_x[...] = jnp.zeros_like(halo_x)
        halo_bc[...] = jnp.zeros_like(halo_bc)

    for b in range(blocks):
        before = halo_bc[...] if b == 0 else bc_ref[b * SPAN - RIM : b * SPAN]
        bc = conv_silu(before, bc_ref[b * SPAN : (b + 1) * SPAN], cbc_ref[...])
        b_f = bc[:, :state].astype(BF16)
        c_f = bc[:, state:].astype(BF16)
        b_t[b] = bc[:, :state].T.astype(BF16)
        c_mat[b] = c_f
        sc = lax.dot_general(c_f, b_f, (((1,), (1,)), ((), ())), preferred_element_type=F32)
        score[b] = jnp.where(r_id >= c_id, sc, 0.0)

    def y_copy(c):
        return send(y_send.at[c], y_recv.at[c], ys_sem.at[c], yr_sem.at[c], pair)

    def z_copy(c):
        return send(z_send.at[c], z_recv.at[c], zs_sem.at[c], zr_sem.at[c], ahead)

    def state_chunk(c, carry):
        lanes = pl.ds(pl.multiple_of(c * LANES, LANES), LANES)
        held = jnp.zeros((state, LANES), F32)
        for b in range(blocks):
            before = halo_x[:, lanes] if b == 0 else x_ref[pl.ds(b * SPAN - RIM, RIM), lanes]
            xc = conv_silu(before, x_ref[pl.ds(b * SPAN, SPAN), lanes], cx_ref[:, lanes]).astype(BF16)
            xconv[pl.ds(b * SPAN, SPAN), lanes] = xc
            tail = jnp.dot(t_split[b], pick_tail[:, lanes], preferred_element_type=F32)
            weighted = (xc.astype(F32) * tail).astype(BF16)
            local_in[b, :, lanes] = held
            new = jnp.dot(b_t[b], weighted, preferred_element_type=F32)
            held = decay_blk[b, 0:1, lanes] * held + new
        final[:, lanes] = held
        y_send[c] = held.astype(BF16)
        y_copy(c).start()
        return carry

    lax.fori_loop(0, chunks, state_chunk, 0)
    dec_copy.wait_recv()
    is_odd = odd.astype(F32)

    def serve(c):
        lanes = pl.ds(pl.multiple_of(c * LANES, LANES), LANES)
        y_copy(c).wait_recv()
        own = final[:, lanes]
        other = y_recv[c].astype(F32)
        d_own = decay_own[0:1, lanes]
        d_other = decay_other[0:1, lanes]
        enter[:, lanes] = is_odd * other

        @pl.when(place > 0)
        def _():
            z_copy(c).wait_recv()
            enter[:, lanes] += z_recv[c].astype(F32) * (1.0 - is_odd + is_odd * d_other)

        @pl.when(place < rows - 1)
        def _():
            both = own * (is_odd + (1.0 - is_odd) * d_other) + other * (1.0 - is_odd + is_odd * d_own)
            final[:, lanes] = both

            @pl.when(place > 0)
            def _():
                final[:, lanes] += d_own * d_other * z_recv[c].astype(F32)

            z_send[c] = final[:, lanes].astype(BF16)
            z_copy(c).start()

    half = lax.broadcasted_iota(jnp.int32, (1, 2 * width), 1) < width
    left = jnp.where(half, 1.0, 0.0).astype(BF16)
    right = jnp.where(half, 0.0, 1.0).astype(BF16)

    def intra(c):
        def one(b, carry):
            token = pl.ds(pl.multiple_of(b * SPAN, SPAN), SPAN)
            head = pl.ds(pl.multiple_of(c * per, per), per)
            lds = ld_row[b, head, :]
            sts = st_row[b, head, :]
            cols = ld_col[b, c]
            sc = score[b]
            for j in range(per // 2):
                lanes = pl.ds(pl.multiple_of(c * LANES + j * 2 * width, 2 * width), 2 * width)
                mixes = []
                for h in (2 * j, 2 * j + 1):
                    gap = jnp.minimum(cols[:, h : h + 1] - lds[h : h + 1], 0.0)
                    mixes.append((sc * jnp.exp(gap) * sts[h : h + 1]).astype(BF16))
                xc = xconv[token, lanes]
                y_ref[token, lanes] = jnp.dot(
                    jnp.concatenate(mixes, 1),
                    jnp.concatenate([xc * left, xc * right], 0),
                    preferred_element_type=F32,
                )
            return carry

        lax.fori_loop(0, blocks, one, 0)

    def slot(j, carry):
        c = j - place

        @pl.when((c >= 0) & (c < chunks))
        def _():
            serve(c)

        @pl.when(j < chunks)
        def _():
            intra(j)

        return carry

    lax.fori_loop(0, chunks + rows - 1, slot, 0)

    def finish(b, carry):
        token = pl.ds(pl.multiple_of(b * SPAN, SPAN), SPAN)
        power = jnp.zeros((SPAN, 1), F32)
        for c in range(chunks):
            lanes = pl.ds(c * LANES, LANES)
            grown = jnp.dot(t_split[b], pick_exp[:, lanes], preferred_element_type=F32)
            ent = (local_in[b, :, lanes] + decay_in[b, 0:1, lanes] * enter[:, lanes]).astype(BF16)
            read = jnp.dot(c_mat[b], ent, preferred_element_type=F32)
            total = y_ref[token, lanes] + grown * read + skip_row[0:1, lanes] * xconv[token, lanes].astype(F32)
            gated = total * half_tanh_silu(z_ref[token, lanes].astype(F32))
            y_ref[token, lanes] = gated
            power = power + jnp.sum(gated * gated, axis=1, keepdims=True)
        scale = lax.rsqrt(power * (1.0 / inner) + 1e-05)
        for c in range(chunks):
            lanes = pl.ds(c * LANES, LANES)
            out_ref[token, lanes] = (y_ref[token, lanes] * scale * gain_ref[:, lanes]).astype(BF16)
        return carry

    lax.fori_loop(0, blocks, finish, 0)

    dec_copy.wait_send()

    @pl.when(q < n_seq - 1)
    def _():
        for copy in halo_copies:
            copy.wait_send()

    def drain(c, carry):
        y_copy(c).wait_send()

        @pl.when(place < rows - 1)
        def _():
            z_copy(c).wait_send()

        return carry

    lax.fori_loop(0, chunks, drain, 0)


def project_kernel(
    n_ref, w_ref, out_ref, w_buf, s1, r1, s2, r2, s3, r3, keep,
    w_sem, s1s, s1r, s2s, s2r, s3s, s3r,
):
    h = lax.axis_index("head")
    core = lax.rem(h, 2)
    side = h // 2
    near = 2 * side + 1 - core
    far = 2 * (1 - side) + core
    cross = 3 - h
    pieces, cols = w_buf.shape[0] // 4, w_buf.shape[2]

    def fetch(block, c, slot):
        start = pl.multiple_of((block * pieces + c) * cols, cols)
        return pltpu.make_async_copy(w_ref.at[:, pl.ds(start, cols)], w_buf.at[slot], w_sem.at[slot])

    def fetch_first(c, carry):
        fetch(cross, c, 2 * c).start()
        fetch(far, c, 2 * c + 1).start()
        return carry

    def fetch_second(c, carry):
        fetch(near, c, 2 * pieces + 2 * c).start()
        fetch(h, c, 2 * pieces + 2 * c + 1).start()
        return carry

    lax.fori_loop(0, pieces, fetch_first, 0)
    lax.fori_loop(0, pieces, fetch_second, 0)

    barrier = pltpu.get_barrier_semaphore()
    for other in (near, far):
        pl.semaphore_signal(barrier, inc=1, device_id={"head": other}, device_id_type=MESH)
    pl.semaphore_wait(barrier, 2)

    def send(src, dst, s, r, to, c):
        return pltpu.make_async_remote_copy(
            src_ref=src.at[c], dst_ref=dst.at[c], send_sem=s.at[c], recv_sem=r.at[c],
            device_id={"head": to}, device_id_type=MESH,
        )

    def tile(block, c, slot):
        fetch(block, c, slot).wait()
        return jnp.dot(n_ref[...], w_buf[slot], preferred_element_type=F32)

    def first(c, carry):
        s1[c] = tile(cross, c, 2 * c).astype(BF16)
        send(s1, r1, s1s, s1r, near, c).start()
        keep[c] = tile(far, c, 2 * c + 1)
        send(s1, r1, s1s, s1r, near, c).wait_recv()
        s2[c] = (keep[c] + r1[c].astype(F32)).astype(BF16)
        send(s2, r2, s2s, s2r, far, c).start()
        return carry

    def second(c, carry):
        s3[c] = tile(near, c, 2 * pieces + 2 * c).astype(BF16)
        send(s3, r3, s3s, s3r, near, c).start()
        keep[c] = tile(h, c, 2 * pieces + 2 * c + 1)
        return carry

    def third(c, carry):
        send(s3, r3, s3s, s3r, near, c).wait_recv()
        send(s2, r2, s2s, s2r, far, c).wait_recv()
        total = keep[c] + r3[c].astype(F32) + r2[c].astype(F32)
        out_ref[pl.ds(pl.multiple_of(c * cols, cols), cols), :] = total.T.astype(BF16)
        return carry

    def drain(c, carry):
        send(s1, r1, s1s, s1r, near, c).wait_send()
        send(s2, r2, s2s, s2r, far, c).wait_send()
        send(s3, r3, s3s, s3r, near, c).wait_send()
        return carry

    lax.fori_loop(0, pieces, first, 0)
    lax.fori_loop(0, pieces, second, 0)
    lax.fori_loop(0, pieces, third, 0)
    lax.fori_loop(0, pieces, drain, 0)


def on_device(n_seq, x_in, bc_in, z_in, dt_raw, a_log, conv_x, conv_bc, d_skip, norm_gain, out_weight):
    tokens, inner = x_in.shape
    heads = dt_raw.shape[0]
    features = out_weight.shape[1]
    state = bc_in.shape[2] // 2
    blocks = tokens // SPAN
    chunks = inner // LANES
    per = heads // chunks
    vmem = pl.BlockSpec(memory_space=pltpu.VMEM)
    dma = pltpu.SemaphoreType.DMA
    normed = pl.pallas_call(
        functools.partial(scan_kernel, n_seq),
        name="scan",
        out_shape=jax.ShapeDtypeStruct((tokens, inner), BF16),
        in_specs=[vmem] * 9,
        out_specs=vmem,
        scratch_shapes=[
            pltpu.VMEM((RIM, inner), BF16),
            pltpu.VMEM((RIM, 2 * state), BF16),
            pltpu.VMEM((tokens, inner), BF16),
            pltpu.VMEM((blocks, state, SPAN), BF16),
            pltpu.VMEM((blocks, SPAN, state), BF16),
            pltpu.VMEM((blocks, SPAN, SPAN), F32),
            pltpu.VMEM((blocks, heads, SPAN), F32),
            pltpu.VMEM((blocks, heads, SPAN), F32),
            pltpu.VMEM((blocks, chunks, SPAN, per), F32),
            pltpu.VMEM((blocks, SPAN, 2 * SPAN), BF16),
            pltpu.VMEM((2 * SPAN, inner), BF16),
            pltpu.VMEM((2 * SPAN, inner), BF16),
            pltpu.VMEM((blocks, 8, inner), F32),
            pltpu.VMEM((blocks, 8, inner), F32),
            pltpu.VMEM((8, inner), F32),
            pltpu.VMEM((8, inner), F32),
            pltpu.VMEM((8, inner), F32),
            pltpu.VMEM((blocks, state, inner), F32),
            pltpu.VMEM((state, inner), F32),
            pltpu.VMEM((tokens, inner), F32),
            pltpu.VMEM((state, inner), F32),
            pltpu.VMEM((chunks, state, LANES), BF16),
            pltpu.VMEM((chunks, state, LANES), BF16),
            pltpu.VMEM((chunks, state, LANES), BF16),
            pltpu.VMEM((chunks, state, LANES), BF16),
            dma((4,)),
            dma((2,)),
            dma((chunks,)),
            dma((chunks,)),
            dma((chunks,)),
            dma((chunks,)),
        ],
        compiler_params=pltpu.CompilerParams(
            collective_id=0, has_side_effects=True, vmem_limit_bytes=48 * 2**20
        ),
    )(
        x_in,
        bc_in.reshape(tokens, 2 * state),
        z_in,
        dt_raw,
        a_log.reshape(1, heads),
        conv_x,
        conv_bc.reshape(conv_bc.shape[0], 2 * state),
        d_skip.reshape(1, heads),
        norm_gain.reshape(1, inner),
    )
    share = features // 4
    cols = min(256, share)
    pieces = share // cols
    part = pltpu.VMEM((pieces, tokens, cols), BF16)
    return pl.pallas_call(
        project_kernel,
        name="project",
        out_shape=jax.ShapeDtypeStruct((share, tokens), BF16),
        in_specs=[vmem, pl.BlockSpec(memory_space=pl.ANY)],
        out_specs=vmem,
        scratch_shapes=[pltpu.VMEM((4 * pieces, inner, cols), BF16)]
        + [part] * 6
        + [pltpu.VMEM((pieces, tokens, cols), F32), dma((4 * pieces,))]
        + [dma((pieces,))] * 6,
        compiler_params=pltpu.CompilerParams(
            collective_id=1, has_side_effects=True, vmem_limit_bytes=48 * 2**20
        ),
    )(normed, out_weight)


def solution(mesh):
    placed = (
        P("seq", "head"),
        P("seq", "head", None),
        P("seq", "head"),
        P("head", "seq"),
        P("head"),
        P(None, "head"),
        P(None, "head", None),
        P("head"),
        P("head"),
        P("head", None),
    )
    return jax.shard_map(
        functools.partial(on_device, mesh.shape["seq"]),
        mesh=mesh, in_specs=placed, out_specs=P("head", "seq"), check_vma=False,
    )
```

```python
import functools

import jax
import jax.numpy as jnp
from jax import lax
from jax.experimental import pallas as pl
from jax.experimental.pallas import tpu as pltpu
from jax.sharding import PartitionSpec as P

SPAN = 128
MESH = pl.DeviceIdType.MESH
F32 = jnp.float32
BF16 = jnp.bfloat16
LANES = 256
RIM = 16


def half_tanh_silu(u):
    return 0.5 * u * (1.0 + jnp.tanh(0.5 * u))


def conv_silu(before, now, taps):
    cat = jnp.concatenate([before.astype(F32), now.astype(F32)], 0)
    width = taps.shape[0]
    total = taps[width - 1 : width] * cat[RIM:]
    for k in range(width - 1):
        total = total + taps[k : k + 1] * pltpu.roll(cat, width - 1 - k, 0)[RIM:]
    return half_tanh_silu(total)


def layer_kernel(
    n_seq, x_hbm, bc_hbm, z_hbm, dt_hbm, alog_hbm, cx_hbm, cbc_hbm, skip_hbm, gain_hbm, w_hbm, out_hbm,
    x_ref, bc_ref, z_ref, dt_ref, alog_ref, cx_ref, cbc_ref, skip_ref, gain_ref, w_buf,
    halo_x, halo_bc, xconv, b_t, c_mat, score, ld_row, st_row, ld_col, t_tail, t_exp, pick,
    decay_in, decay_blk, decay_own, decay_other, skip_row, local_in, final, y_ref, enter,
    y_send, y_recv, z_send, z_recv, n_buf, s1, r1, s2, r2, s3, r3, keep, o_buf,
    in_sem, w_sem, halo_sems, dec_sems, ys_sem, yr_sem, zs_sem, zr_sem,
    s1s, s1r, s2s, s2r, s3s, s3r, o_sem,
):
    tokens, inner = x_ref.shape
    heads = dt_ref.shape[0]
    state = b_t.shape[1]
    width = inner // heads
    blocks = tokens // SPAN
    chunks = inner // LANES
    per = heads // chunks
    rows = n_seq // 2
    pieces, cols = keep.shape[0], keep.shape[2]
    half = tokens // 2
    q = lax.axis_index("seq")
    odd = lax.rem(q, 2)
    place = q // 2
    pair = q + 1 - 2 * odd
    after = lax.rem(q + 1, n_seq)
    ahead = lax.rem(q + 2, n_seq)
    h = lax.axis_index("head")
    core = lax.rem(h, 2)
    side = h // 2
    near = 2 * side + 1 - core
    far = 2 * (1 - side) + core
    cross = 3 - h

    loads = [
        pltpu.make_async_copy(src, dst, in_sem.at[i])
        for i, (src, dst) in enumerate(
            [
                (dt_hbm, dt_ref), (alog_hbm, alog_ref), (skip_hbm, skip_ref), (bc_hbm, bc_ref), (cbc_hbm, cbc_ref),
                (cx_hbm, cx_ref), (x_hbm, x_ref), (gain_hbm, gain_ref), (z_hbm, z_ref),
            ]
        )
    ]
    for load in loads:
        load.start()

    barrier = pltpu.get_barrier_semaphore()
    pl.semaphore_signal(barrier, inc=1, device_id={"seq": pair}, device_id_type=MESH)
    for other in (near, far):
        pl.semaphore_signal(barrier, inc=1, device_id={"head": other}, device_id_type=MESH)

    @pl.when(q > 0)
    def _():
        pl.semaphore_signal(barrier, inc=1, device_id={"seq": q - 1}, device_id_type=MESH)

    @pl.when(q > 1)
    def _():
        pl.semaphore_signal(barrier, inc=1, device_id={"seq": q - 2}, device_id_type=MESH)

    def fetch(block, c, slot):
        start = pl.multiple_of((block * pieces + c) * cols, cols)
        return pltpu.make_async_copy(w_hbm.at[:, pl.ds(start, cols)], w_buf.at[slot], w_sem.at[slot])

    def fetch_all(act):
        def one(c, carry):
            act(fetch(cross, c, c))
            act(fetch(far, c, pieces + c))
            act(fetch(near, c, 2 * pieces + c))
            act(fetch(h, c, 3 * pieces + c))
            return carry

        lax.fori_loop(0, pieces, one, 0)

    fetch_all(lambda copy: copy.start())

    peers = 3 + jnp.minimum(n_seq - 1 - q, 1) + jnp.minimum(jnp.maximum(n_seq - 2 - q, 0), 1)
    pl.semaphore_wait(barrier, peers)

    def send(src, dst, s, r, to):
        return pltpu.make_async_remote_copy(
            src_ref=src, dst_ref=dst, send_sem=s, recv_sem=r, device_id=to, device_id_type=MESH
        )

    halo_copies = [
        send(bc_hbm.at[pl.ds(tokens - RIM, RIM)], halo_bc, halo_sems.at[2], halo_sems.at[3], {"seq": after}),
        send(x_hbm.at[pl.ds(tokens - RIM, RIM)], halo_x, halo_sems.at[0], halo_sems.at[1], {"seq": after}),
    ]

    @pl.when(q < n_seq - 1)
    def _():
        for copy in halo_copies:
            copy.start()

    r_id = lax.broadcasted_iota(jnp.int32, (SPAN, SPAN), 0)
    c_id = lax.broadcasted_iota(jnp.int32, (SPAN, SPAN), 1)
    upto = jnp.where(r_id <= c_id, 1.0, 0.0).astype(F32)
    hr = lax.broadcasted_iota(jnp.int32, (heads, heads), 0)
    hc = lax.broadcasted_iota(jnp.int32, (heads, heads), 1)
    lane_head = lax.shift_right_logical(
        lax.broadcasted_iota(jnp.int32, (heads, inner), 1), jnp.full((heads, inner), width.bit_length() - 1, jnp.int32)
    )
    mine = lax.broadcasted_iota(jnp.int32, (heads, inner), 0) == lane_head
    ones = jnp.where(mine, 1.0, 0.0).astype(F32)
    pick[...] = jnp.concatenate([ones, ones], 0).astype(BF16)
    for load in loads[:3]:
        load.wait()
    neg_a = -jnp.sum(jnp.where(hr == hc, jnp.exp(alog_ref[...]), 0.0), axis=1, keepdims=True)
    skips = jnp.sum(jnp.where(hr == hc, jnp.broadcast_to(skip_ref[...], (heads, heads)), 0.0), axis=1, keepdims=True)
    skip_row[...] = jnp.broadcast_to(jnp.sum(ones * skips, axis=0, keepdims=True), (8, inner))
    dt = jnp.concatenate([dt_ref[:, b * SPAN : (b + 1) * SPAN].astype(F32) for b in range(blocks)], 0)
    e = jnp.exp(-jnp.abs(dt))
    log1p = jnp.where(e < 0.01, e * (1.0 - e * (0.5 - e * (1.0 / 3.0 - 0.25 * e))), jnp.log(1.0 + e))
    step = jnp.maximum(dt, 0.0) + log1p
    rate = jnp.concatenate([neg_a] * blocks, 0) * step
    ld = jnp.dot(rate, upto, preferred_element_type=F32, precision=lax.Precision.HIGHEST)
    tail = jnp.exp(ld[:, SPAN - 1 : SPAN] - ld) * step
    grow = jnp.exp(ld)

    def turned_pieces(value):
        high = value.astype(BF16).astype(F32)
        low = value - high
        parts = []
        for b in range(blocks):
            parts += [high[b * heads : (b + 1) * heads], low[b * heads : (b + 1) * heads]]
        turned = jnp.concatenate(parts, 0).T
        return [turned[:, 2 * heads * b : 2 * heads * (b + 1)].astype(BF16) for b in range(blocks)]

    tails, grows, turned = turned_pieces(tail), turned_pieces(grow), ld.T
    running = jnp.ones((8, inner), F32)
    for b in range(blocks):
        t_tail[b] = tails[b]
        t_exp[b] = grows[b]
        for c in range(chunks):
            at = b * heads + c * per
            ld_row[b, c] = ld[at : at + per]
            st_row[b, c] = step[at : at + per]
            ld_col[b, c] = turned[:, at : at + per]
        last = jnp.sum(ones * grow[b * heads : (b + 1) * heads, SPAN - 1 : SPAN], axis=0, keepdims=True)
        decay_in[b] = running
        decay_blk[b] = jnp.broadcast_to(last, (8, inner))
        running = running * last
    decay_own[...] = running
    dec_copy = send(decay_own, decay_other, dec_sems.at[0], dec_sems.at[1], {"seq": pair})
    dec_copy.start()
    for load in loads[3:7]:
        load.wait()

    @pl.when(q > 0)
    def _():
        for copy in halo_copies:
            copy.wait_recv()

    @pl.when(q == 0)
    def _():
        halo_x[...] = jnp.zeros_like(halo_x)
        halo_bc[...] = jnp.zeros_like(halo_bc)

    for b in range(blocks):
        before = halo_bc[...] if b == 0 else bc_ref[b * SPAN - RIM : b * SPAN]
        bc = conv_silu(before, bc_ref[b * SPAN : (b + 1) * SPAN], cbc_ref[...])
        b_f = bc[:, :state].astype(BF16)
        c_f = bc[:, state:].astype(BF16)
        b_t[b] = bc[:, :state].T.astype(BF16)
        c_mat[b] = c_f
        sc = lax.dot_general(c_f, b_f, (((1,), (1,)), ((), ())), preferred_element_type=F32)
        score[b] = jnp.where(r_id >= c_id, sc, 0.0)

    def y_copy(c):
        return send(y_send.at[c], y_recv.at[c], ys_sem.at[c], yr_sem.at[c], {"seq": pair})

    def z_copy(c):
        return send(z_send.at[c], z_recv.at[c], zs_sem.at[c], zr_sem.at[c], {"seq": ahead})

    def state_chunk(c, carry):
        lanes = pl.ds(pl.multiple_of(c * LANES, LANES), LANES)
        held = jnp.zeros((state, LANES), F32)
        for b in range(blocks):
            tail = jnp.dot(t_tail[b], pick[:, lanes], preferred_element_type=F32)
            before = halo_x[:, lanes] if b == 0 else x_ref[pl.ds(b * SPAN - RIM, RIM), lanes]
            xc = conv_silu(before, x_ref[pl.ds(b * SPAN, SPAN), lanes], cx_ref[:, lanes]).astype(BF16)
            xconv[pl.ds(b * SPAN, SPAN), lanes] = xc
            weighted = (xc.astype(F32) * tail).astype(BF16)
            local_in[b, :, lanes] = held
            new = jnp.dot(b_t[b], weighted, preferred_element_type=F32)
            held = decay_blk[b, 0:1, lanes] * held + new
        final[:, lanes] = held
        y_send[c] = held.astype(BF16)
        y_copy(c).start()
        return carry

    lax.fori_loop(0, chunks, state_chunk, 0)
    dec_copy.wait_recv()
    is_odd = odd.astype(F32)

    def serve(c):
        lanes = pl.ds(pl.multiple_of(c * LANES, LANES), LANES)
        y_copy(c).wait_recv()
        own = final[:, lanes]
        other = y_recv[c].astype(F32)
        d_own = decay_own[0:1, lanes]
        d_other = decay_other[0:1, lanes]
        enter[:, lanes] = is_odd * other

        @pl.when(place < rows - 1)
        def _():
            final[:, lanes] = own * (is_odd + (1.0 - is_odd) * d_other) + other * (1.0 - is_odd + is_odd * d_own)

        @pl.when(place > 0)
        def _():
            z_copy(c).wait_recv()

            @pl.when(place < rows - 1)
            def _():
                final[:, lanes] += d_own * d_other * z_recv[c].astype(F32)

        @pl.when(place < rows - 1)
        def _():
            z_send[c] = final[:, lanes].astype(BF16)
            z_copy(c).start()

        @pl.when(place > 0)
        def _():
            enter[:, lanes] += z_recv[c].astype(F32) * (1.0 - is_odd + is_odd * d_other)

    first_head = lax.broadcasted_iota(jnp.int32, (1, 2 * width), 1) < width
    left = jnp.where(first_head, 1.0, 0.0).astype(BF16)
    right = jnp.where(first_head, 0.0, 1.0).astype(BF16)

    def intra(c):
        for b in range(blocks):
            token = pl.ds(b * SPAN, SPAN)
            lds = ld_row[b, c]
            sts = st_row[b, c]
            cl = ld_col[b, c]
            for j in range(per // 2):
                lanes = pl.ds(pl.multiple_of(c * LANES + j * 2 * width, 2 * width), 2 * width)
                mixes = []
                for i in (2 * j, 2 * j + 1):
                    gap = jnp.minimum(cl[:, i : i + 1] - lds[i : i + 1], 0.0)
                    mixes.append((score[b] * jnp.exp(gap) * sts[i : i + 1]).astype(BF16))
                xc = xconv[token, lanes]
                y_ref[token, lanes] = jnp.dot(
                    jnp.concatenate(mixes, 1),
                    jnp.concatenate([xc * left, xc * right], 0),
                    preferred_element_type=F32,
                )

    def slot(j, carry):
        c = j - place

        @pl.when((c >= 0) & (c < chunks))
        def _():
            serve(c)

        @pl.when(j < chunks)
        def _():
            intra(j)

        return carry

    lax.fori_loop(0, chunks + rows - 1, slot, 0)
    for load in loads[7:]:
        load.wait()
    fetch_all(lambda copy: copy.wait())

    def finish(b, carry):
        token = pl.ds(pl.multiple_of(b * SPAN, SPAN), SPAN)
        power = jnp.zeros((SPAN, 1), F32)
        for c in range(chunks):
            lanes = pl.ds(c * LANES, LANES)
            grown = jnp.dot(t_exp[b], pick[:, lanes], preferred_element_type=F32)
            ent = (local_in[b, :, lanes] + decay_in[b, 0:1, lanes] * enter[:, lanes]).astype(BF16)
            read = jnp.dot(c_mat[b], ent, preferred_element_type=F32)
            total = y_ref[token, lanes] + grown * read + skip_row[0:1, lanes] * xconv[token, lanes].astype(F32)
            gated = total * half_tanh_silu(z_ref[token, lanes].astype(F32))
            y_ref[token, lanes] = gated
            power = power + jnp.sum(gated * gated, axis=1, keepdims=True)
        scale = lax.rsqrt(power * (1.0 / inner) + 1e-05)
        for c in range(chunks):
            lanes = pl.ds(c * LANES, LANES)
            n_buf[token, lanes] = (y_ref[token, lanes] * scale * gain_ref[:, lanes]).astype(BF16)
        return carry

    def near_copy(src, dst, s, r, i):
        return send(src.at[i], dst.at[i], s.at[i], r.at[i], {"head": near})

    def far_copy(i):
        return send(s2.at[i], r2.at[i], s2s.at[i], s2r.at[i], {"head": far})

    def first(part, c):
        i = part * pieces + c
        token = pl.ds(pl.multiple_of(part * half, half), half)
        s1[i] = jnp.dot(n_buf[token, :], w_buf[c], preferred_element_type=F32).astype(BF16)
        near_copy(s1, r1, s1s, s1r, i).start()
        summed = jnp.dot(n_buf[token, :], w_buf[pieces + c], preferred_element_type=F32)
        near_copy(s1, r1, s1s, s1r, i).wait_recv()
        s2[i] = (summed + r1[i].astype(F32)).astype(BF16)
        far_copy(i).start()

    def one_half(part, carry):
        lax.fori_loop(part * (blocks // 2), (part + 1) * (blocks // 2), finish, 0)

        def piece(c, carry):
            first(part, c)
            return carry

        return lax.fori_loop(0, pieces, piece, carry)

    def second(c, carry):
        s3[c] = jnp.dot(n_buf[...], w_buf[2 * pieces + c], preferred_element_type=F32).astype(BF16)
        near_copy(s3, r3, s3s, s3r, c).start()
        keep[c] = jnp.dot(n_buf[...], w_buf[3 * pieces + c], preferred_element_type=F32)
        return carry

    def third(c, carry):
        near_copy(s3, r3, s3s, s3r, c).wait_recv()
        keep[c] += r3[c].astype(F32)
        return carry

    def store(part, c):
        place_out = (
            pl.ds(pl.multiple_of(c * cols, cols), cols),
            pl.ds(pl.multiple_of(part * half, half), half),
        )
        return pltpu.make_async_copy(
            o_buf.at[part * pieces + c], out_hbm.at[place_out[0], place_out[1]], o_sem.at[part * pieces + c]
        )

    def fourth(part, carry):
        def piece(c, carry):
            i = part * pieces + c
            far_copy(i).wait_recv()
            total = keep[c, pl.ds(pl.multiple_of(part * half, half), half), :] + r2[i].astype(F32)
            o_buf[i] = total.T.astype(BF16)
            store(part, c).start()
            return carry

        return lax.fori_loop(0, pieces, piece, carry)

    lax.fori_loop(0, 2, one_half, 0)
    lax.fori_loop(0, pieces, second, 0)
    lax.fori_loop(0, pieces, third, 0)
    lax.fori_loop(0, 2, fourth, 0)

    dec_copy.wait_send()

    @pl.when(q < n_seq - 1)
    def _():
        for copy in halo_copies:
            copy.wait_send()

    def drain_state(c, carry):
        y_copy(c).wait_send()

        @pl.when(place < rows - 1)
        def _():
            z_copy(c).wait_send()

        return carry

    def drain_first(i, carry):
        near_copy(s1, r1, s1s, s1r, i).wait_send()
        far_copy(i).wait_send()
        return carry

    def drain_second(c, carry):
        near_copy(s3, r3, s3s, s3r, c).wait_send()
        store(0, c).wait()
        store(1, c).wait()
        return carry

    lax.fori_loop(0, chunks, drain_state, 0)
    lax.fori_loop(0, 2 * pieces, drain_first, 0)
    lax.fori_loop(0, pieces, drain_second, 0)


def on_device(n_seq, x_in, bc_in, z_in, dt_raw, a_log, conv_x, conv_bc, d_skip, norm_gain, out_weight):
    tokens, inner = x_in.shape
    heads = dt_raw.shape[0]
    features = out_weight.shape[1]
    state = bc_in.shape[2] // 2
    taps = conv_x.shape[0]
    blocks = tokens // SPAN
    chunks = inner // LANES
    per = heads // chunks
    share = features // 4
    cols = min(256, share)
    pieces = share // cols
    hbm = pl.BlockSpec(memory_space=pl.ANY)
    dma = pltpu.SemaphoreType.DMA
    vmem = pltpu.VMEM
    halves = vmem((2 * pieces, tokens // 2, cols), BF16)
    wholes = vmem((pieces, tokens, cols), BF16)
    moved = vmem((chunks, state, LANES), BF16)
    return pl.pallas_call(
        functools.partial(layer_kernel, n_seq),
        name="layer",
        out_shape=jax.ShapeDtypeStruct((share, tokens), BF16),
        in_specs=[hbm] * 10,
        out_specs=hbm,
        scratch_shapes=[
            vmem((tokens, inner), BF16),
            vmem((tokens, 2 * state), BF16),
            vmem((tokens, inner), BF16),
            vmem((heads, tokens), BF16),
            vmem((1, heads), F32),
            vmem((taps, inner), F32),
            vmem((taps, 2 * state), F32),
            vmem((1, heads), F32),
            vmem((1, inner), F32),
            vmem((4 * pieces, inner, cols), BF16),
            vmem((RIM, inner), BF16),
            vmem((RIM, 2 * state), BF16),
            vmem((tokens, inner), BF16),
            vmem((blocks, state, SPAN), BF16),
            vmem((blocks, SPAN, state), BF16),
            vmem((blocks, SPAN, SPAN), F32),
            vmem((blocks, chunks, per, SPAN), F32),
            vmem((blocks, chunks, per, SPAN), F32),
            vmem((blocks, chunks, SPAN, per), F32),
            vmem((blocks, SPAN, 2 * heads), BF16),
            vmem((blocks, SPAN, 2 * heads), BF16),
            vmem((2 * heads, inner), BF16),
            vmem((blocks, 8, inner), F32),
            vmem((blocks, 8, inner), F32),
            vmem((8, inner), F32),
            vmem((8, inner), F32),
            vmem((8, inner), F32),
            vmem((blocks, state, inner), F32),
            vmem((state, inner), F32),
            vmem((tokens, inner), F32),
            vmem((state, inner), F32),
            moved,
            moved,
            moved,
            moved,
            vmem((tokens, inner), BF16),
            halves,
            halves,
            halves,
            halves,
            wholes,
            wholes,
            vmem((pieces, tokens, cols), F32),
            vmem((2 * pieces, cols, tokens // 2), BF16),
            dma((9,)),
            dma((4 * pieces,)),
            dma((4,)),
            dma((2,)),
            dma((chunks,)),
            dma((chunks,)),
            dma((chunks,)),
            dma((chunks,)),
            dma((2 * pieces,)),
            dma((2 * pieces,)),
            dma((2 * pieces,)),
            dma((2 * pieces,)),
            dma((pieces,)),
            dma((pieces,)),
            dma((2 * pieces,)),
        ],
        compiler_params=pltpu.CompilerParams(
            collective_id=0, has_side_effects=True, vmem_limit_bytes=60 * 2**20
        ),
    )(
        x_in,
        bc_in.reshape(tokens, 2 * state),
        z_in,
        dt_raw,
        a_log.reshape(1, heads),
        conv_x,
        conv_bc.reshape(taps, 2 * state),
        d_skip.reshape(1, heads),
        norm_gain.reshape(1, inner),
        out_weight,
    )


def solution(mesh):
    placed = (
        P("seq", "head"),
        P("seq", "head", None),
        P("seq", "head"),
        P("head", "seq"),
        P("head"),
        P(None, "head"),
        P(None, "head", None),
        P("head"),
        P("head"),
        P("head", None),
    )
    return jax.shard_map(
        functools.partial(on_device, mesh.shape["seq"]),
        mesh=mesh, in_specs=placed, out_specs=P("head", "seq"), check_vma=False,
    )
```

```python
import functools

import jax
import jax.numpy as jnp
from jax import lax
from jax.experimental import pallas as pl
from jax.experimental.pallas import tpu as pltpu
from jax.sharding import PartitionSpec as P

SPAN = 128
MESH = pl.DeviceIdType.MESH
F32 = jnp.float32
BF16 = jnp.bfloat16
LANES = 256
RIM = 16


def half_tanh_silu(u):
    return 0.5 * u * (1.0 + jnp.tanh(0.5 * u))


def conv_silu(before, now, taps):
    cat = jnp.concatenate([before.astype(F32), now.astype(F32)], 0)
    width = taps.shape[0]
    total = taps[width - 1 : width] * cat[RIM:]
    for k in range(width - 1):
        total = total + taps[k : k + 1] * pltpu.roll(cat, width - 1 - k, 0)[RIM:]
    return half_tanh_silu(total)


def layer_kernel(
    n_seq, x_hbm, bc_hbm, z_hbm, dt_hbm, alog_hbm, cx_hbm, cbc_hbm, skip_hbm, gain_hbm, w_hbm, out_ref,
    x_ref, bc_ref, z_ref, dt_ref, alog_ref, cx_ref, cbc_ref, skip_ref, gain_ref, w_buf,
    halo_x, halo_bc, xconv, b_t, c_mat, score, ld_row, st_row, ld_col, t_tail, t_exp, pick,
    decay_in, decay_blk, decay_own, decay_other, skip_row, local_in, final, y_ref, enter,
    y_send, y_recv, z_send, z_recv, n_buf, s1, r1, s2, r2, s3, r3, keep,
    in_sem, w_sem, halo_sems, dec_sems, ys_sem, yr_sem, zs_sem, zr_sem,
    s1s, s1r, s2s, s2r, s3s, s3r,
):
    tokens, inner = x_ref.shape
    heads = dt_ref.shape[0]
    state = b_t.shape[1]
    width = inner // heads
    blocks = tokens // SPAN
    chunks = inner // LANES
    per = heads // chunks
    rows = n_seq // 2
    pieces, cols = keep.shape[0], keep.shape[2]
    q = lax.axis_index("seq")
    odd = lax.rem(q, 2)
    place = q // 2
    pair = q + 1 - 2 * odd
    after = lax.rem(q + 1, n_seq)
    ahead = lax.rem(q + 2, n_seq)
    h = lax.axis_index("head")
    core = lax.rem(h, 2)
    side = h // 2
    near = 2 * side + 1 - core
    far = 2 * (1 - side) + core
    cross = 3 - h

    loads = [
        pltpu.make_async_copy(src, dst, in_sem.at[i])
        for i, (src, dst) in enumerate(
            [
                (dt_hbm, dt_ref), (alog_hbm, alog_ref), (skip_hbm, skip_ref), (bc_hbm, bc_ref), (cbc_hbm, cbc_ref),
                (cx_hbm, cx_ref), (x_hbm, x_ref), (gain_hbm, gain_ref), (z_hbm, z_ref),
            ]
        )
    ]
    for load in loads:
        load.start()

    barrier = pltpu.get_barrier_semaphore()
    pl.semaphore_signal(barrier, inc=1, device_id={"seq": pair}, device_id_type=MESH)
    for other in (near, far):
        pl.semaphore_signal(barrier, inc=1, device_id={"head": other}, device_id_type=MESH)

    @pl.when(q > 0)
    def _():
        pl.semaphore_signal(barrier, inc=1, device_id={"seq": q - 1}, device_id_type=MESH)

    @pl.when(q > 1)
    def _():
        pl.semaphore_signal(barrier, inc=1, device_id={"seq": q - 2}, device_id_type=MESH)

    def fetch(block, c, slot):
        start = pl.multiple_of((block * pieces + c) * cols, cols)
        return pltpu.make_async_copy(w_hbm.at[:, pl.ds(start, cols)], w_buf.at[slot], w_sem.at[slot])

    def fetch_all(act):
        def one(c, carry):
            act(fetch(cross, c, c))
            act(fetch(far, c, pieces + c))
            act(fetch(near, c, 2 * pieces + c))
            act(fetch(h, c, 3 * pieces + c))
            return carry

        lax.fori_loop(0, pieces, one, 0)

    peers = 3 + jnp.minimum(n_seq - 1 - q, 1) + jnp.minimum(jnp.maximum(n_seq - 2 - q, 0), 1)
    pl.semaphore_wait(barrier, peers)

    def send(src, dst, s, r, to):
        return pltpu.make_async_remote_copy(
            src_ref=src, dst_ref=dst, send_sem=s, recv_sem=r, device_id=to, device_id_type=MESH
        )

    halo_copies = [
        send(bc_hbm.at[pl.ds(tokens - RIM, RIM)], halo_bc, halo_sems.at[2], halo_sems.at[3], {"seq": after}),
        send(x_hbm.at[pl.ds(tokens - RIM, RIM)], halo_x, halo_sems.at[0], halo_sems.at[1], {"seq": after}),
    ]

    @pl.when(q < n_seq - 1)
    def _():
        for copy in halo_copies:
            copy.start()

    r_id = lax.broadcasted_iota(jnp.int32, (SPAN, SPAN), 0)
    c_id = lax.broadcasted_iota(jnp.int32, (SPAN, SPAN), 1)
    upto = jnp.where(r_id <= c_id, 1.0, 0.0).astype(F32)
    hr = lax.broadcasted_iota(jnp.int32, (heads, heads), 0)
    hc = lax.broadcasted_iota(jnp.int32, (heads, heads), 1)
    lane_head = lax.shift_right_logical(
        lax.broadcasted_iota(jnp.int32, (heads, inner), 1), jnp.full((heads, inner), width.bit_length() - 1, jnp.int32)
    )
    mine = lax.broadcasted_iota(jnp.int32, (heads, inner), 0) == lane_head
    ones = jnp.where(mine, 1.0, 0.0).astype(F32)
    pick[...] = jnp.concatenate([ones, ones], 0).astype(BF16)
    for load in loads[:3]:
        load.wait()
    neg_a = -jnp.sum(jnp.where(hr == hc, jnp.exp(alog_ref[...]), 0.0), axis=1, keepdims=True)
    skips = jnp.sum(jnp.where(hr == hc, jnp.broadcast_to(skip_ref[...], (heads, heads)), 0.0), axis=1, keepdims=True)
    skip_row[...] = jnp.broadcast_to(jnp.sum(ones * skips, axis=0, keepdims=True), (8, inner))
    dt = jnp.concatenate([dt_ref[:, b * SPAN : (b + 1) * SPAN].astype(F32) for b in range(blocks)], 0)
    e = jnp.exp(-jnp.abs(dt))
    log1p = jnp.where(e < 0.01, e * (1.0 - e * (0.5 - e * (1.0 / 3.0 - 0.25 * e))), jnp.log(1.0 + e))
    step = jnp.maximum(dt, 0.0) + log1p
    rate = jnp.concatenate([neg_a] * blocks, 0) * step
    ld = jnp.dot(rate, upto, preferred_element_type=F32, precision=lax.Precision.HIGHEST)
    tail = jnp.exp(ld[:, SPAN - 1 : SPAN] - ld) * step
    grow = jnp.exp(ld)

    def turned_pieces(value):
        high = value.astype(BF16).astype(F32)
        low = value - high
        parts = []
        for b in range(blocks):
            parts += [high[b * heads : (b + 1) * heads], low[b * heads : (b + 1) * heads]]
        turned = jnp.concatenate(parts, 0).T
        return [turned[:, 2 * heads * b : 2 * heads * (b + 1)].astype(BF16) for b in range(blocks)]

    tails, grows, turned = turned_pieces(tail), turned_pieces(grow), ld.T
    running = jnp.ones((8, inner), F32)
    for b in range(blocks):
        t_tail[b] = tails[b]
        t_exp[b] = grows[b]
        for c in range(chunks):
            at = b * heads + c * per
            ld_row[b, c] = ld[at : at + per]
            st_row[b, c] = step[at : at + per]
            ld_col[b, c] = turned[:, at : at + per]
        last = jnp.sum(ones * grow[b * heads : (b + 1) * heads, SPAN - 1 : SPAN], axis=0, keepdims=True)
        decay_in[b] = running
        decay_blk[b] = jnp.broadcast_to(last, (8, inner))
        running = running * last
    decay_own[...] = running
    dec_copy = send(decay_own, decay_other, dec_sems.at[0], dec_sems.at[1], {"seq": pair})
    dec_copy.start()
    for load in loads[3:7]:
        load.wait()
    fetch_all(lambda copy: copy.start())

    @pl.when(q > 0)
    def _():
        for copy in halo_copies:
            copy.wait_recv()

    @pl.when(q == 0)
    def _():
        halo_x[...] = jnp.zeros_like(halo_x)
        halo_bc[...] = jnp.zeros_like(halo_bc)

    taps_bc = jnp.concatenate(
        [cbc_ref[:, k * 2 * state : (k + 1) * 2 * state] for k in range(cx_ref.shape[0])], 0
    )
    for b in range(blocks):
        before = halo_bc[...] if b == 0 else bc_ref[b * SPAN - RIM : b * SPAN]
        bc = conv_silu(before, bc_ref[b * SPAN : (b + 1) * SPAN], taps_bc)
        b_f = bc[:, :state].astype(BF16)
        c_f = bc[:, state:].astype(BF16)
        b_t[b] = bc[:, :state].T.astype(BF16)
        c_mat[b] = c_f
        sc = lax.dot_general(c_f, b_f, (((1,), (1,)), ((), ())), preferred_element_type=F32)
        score[b] = jnp.where(r_id >= c_id, sc, 0.0)

    def y_copy(c):
        return send(y_send.at[c], y_recv.at[c], ys_sem.at[c], yr_sem.at[c], {"seq": pair})

    def z_copy(c):
        return send(z_send.at[c], z_recv.at[c], zs_sem.at[c], zr_sem.at[c], {"seq": ahead})

    def state_chunk(c):
        lanes = pl.ds(pl.multiple_of(c * LANES, LANES), LANES)
        held = jnp.zeros((state, LANES), F32)
        for b in range(blocks):
            tail = jnp.dot(t_tail[b], pick[:, lanes], preferred_element_type=F32)
            before = halo_x[:, lanes] if b == 0 else x_ref[pl.ds(b * SPAN - RIM, RIM), lanes]
            xc = conv_silu(before, x_ref[pl.ds(b * SPAN, SPAN), lanes], cx_ref[:, lanes]).astype(BF16)
            xconv[pl.ds(b * SPAN, SPAN), lanes] = xc
            weighted = (xc.astype(F32) * tail).astype(BF16)
            local_in[b, :, lanes] = held
            new = jnp.dot(b_t[b], weighted, preferred_element_type=F32)
            held = decay_blk[b, 0:1, lanes] * held + new
        final[:, lanes] = held
        y_send[c] = held.astype(BF16)
        y_copy(c).start()

    dec_copy.wait_recv()
    is_odd = odd.astype(F32)

    def serve(c):
        lanes = pl.ds(pl.multiple_of(c * LANES, LANES), LANES)
        y_copy(c).wait_recv()
        own = final[:, lanes]
        other = y_recv[c].astype(F32)
        d_own = decay_own[0:1, lanes]
        d_other = decay_other[0:1, lanes]
        enter[:, lanes] = is_odd * other

        @pl.when(place < rows - 1)
        def _():
            final[:, lanes] = own * (is_odd + (1.0 - is_odd) * d_other) + other * (1.0 - is_odd + is_odd * d_own)

        @pl.when(place > 0)
        def _():
            z_copy(c).wait_recv()

            @pl.when(place < rows - 1)
            def _():
                final[:, lanes] += d_own * d_other * z_recv[c].astype(F32)

        @pl.when(place < rows - 1)
        def _():
            z_send[c] = final[:, lanes].astype(BF16)
            z_copy(c).start()

        @pl.when(place > 0)
        def _():
            enter[:, lanes] += z_recv[c].astype(F32) * (1.0 - is_odd + is_odd * d_other)

    first_head = lax.broadcasted_iota(jnp.int32, (1, 2 * width), 1) < width
    left = jnp.where(first_head, 1.0, 0.0).astype(BF16)
    right = jnp.where(first_head, 0.0, 1.0).astype(BF16)

    def intra(c):
        for b in range(blocks):
            token = pl.ds(b * SPAN, SPAN)
            lds = ld_row[b, c]
            sts = st_row[b, c]
            cl = ld_col[b, c]
            for j in range(per // 2):
                lanes = pl.ds(pl.multiple_of(c * LANES + j * 2 * width, 2 * width), 2 * width)
                mixes = []
                for i in (2 * j, 2 * j + 1):
                    gap = jnp.minimum(cl[:, i : i + 1] - lds[i : i + 1], 0.0)
                    mixes.append((score[b] * jnp.exp(gap) * sts[i : i + 1]).astype(BF16))
                xc = xconv[token, lanes]
                y_ref[token, lanes] = jnp.dot(
                    jnp.concatenate(mixes, 1),
                    jnp.concatenate([xc * left, xc * right], 0),
                    preferred_element_type=F32,
                )

    def slot(j, carry):
        c = j - 2 - 2 * place

        @pl.when((c >= 0) & (c < chunks))
        def _():
            serve(c)

        @pl.when(j < chunks)
        def _():
            state_chunk(j)

        @pl.when((j >= chunks) & (j < 2 * chunks))
        def _():
            intra(j - chunks)

        return carry

    lax.fori_loop(0, max(2 * chunks, chunks + 2 * rows), slot, 0)
    for load in loads[7:]:
        load.wait()
    fetch_all(lambda copy: copy.wait())

    def finish(b):
        token = pl.ds(pl.multiple_of(b * SPAN, SPAN), SPAN)
        power = jnp.zeros((SPAN, 1), F32)
        for c in range(chunks):
            lanes = pl.ds(c * LANES, LANES)
            grown = jnp.dot(t_exp[b], pick[:, lanes], preferred_element_type=F32)
            ent = (local_in[b, :, lanes] + decay_in[b, 0:1, lanes] * enter[:, lanes]).astype(BF16)
            read = jnp.dot(c_mat[b], ent, preferred_element_type=F32)
            total = y_ref[token, lanes] + grown * read + skip_row[0:1, lanes] * xconv[token, lanes].astype(F32)
            gated = total * half_tanh_silu(z_ref[token, lanes].astype(F32))
            y_ref[token, lanes] = gated
            power = power + jnp.sum(gated * gated, axis=1, keepdims=True)
        scale = lax.rsqrt(power * (1.0 / inner) + 1e-05)
        for c in range(chunks):
            lanes = pl.ds(c * LANES, LANES)
            n_buf[token, lanes] = (y_ref[token, lanes] * scale * gain_ref[:, lanes]).astype(BF16)

    def near_copy(src, dst, s, r, i):
        return send(src.at[i], dst.at[i], s.at[i], r.at[i], {"head": near})

    def far_copy(i):
        return send(s2.at[i], r2.at[i], s2s.at[i], s2r.at[i], {"head": far})

    def one_part(part, carry):
        token = pl.ds(pl.multiple_of(part * SPAN, SPAN), SPAN)
        finish(part)

        def pair_piece(c, carry):
            i = part * pieces + c
            s1[i] = jnp.dot(n_buf[token, :], w_buf[c], preferred_element_type=F32).astype(BF16)
            near_copy(s1, r1, s1s, s1r, i).start()
            return carry

        def far_piece(c, carry):
            i = part * pieces + c
            summed = jnp.dot(n_buf[token, :], w_buf[pieces + c], preferred_element_type=F32)
            near_copy(s1, r1, s1s, s1r, i).wait_recv()
            s2[i] = (summed + r1[i].astype(F32)).astype(BF16)
            far_copy(i).start()
            return carry

        lax.fori_loop(0, pieces, pair_piece, 0)
        lax.fori_loop(0, pieces, far_piece, 0)
        return carry

    def second(c, carry):
        s3[c] = jnp.dot(n_buf[...], w_buf[2 * pieces + c], preferred_element_type=F32).astype(BF16)
        near_copy(s3, r3, s3s, s3r, c).start()
        keep[c] = jnp.dot(n_buf[...], w_buf[3 * pieces + c], preferred_element_type=F32)
        return carry

    def third(c, carry):
        near_copy(s3, r3, s3s, s3r, c).wait_recv()
        keep[c] += r3[c].astype(F32)
        return carry

    def fourth(part, carry):
        token = pl.ds(pl.multiple_of(part * SPAN, SPAN), SPAN)

        def piece(c, carry):
            i = part * pieces + c
            far_copy(i).wait_recv()
            total = keep[c, token, :] + r2[i].astype(F32)
            out_ref[pl.ds(pl.multiple_of(c * cols, cols), cols), token] = total.T.astype(BF16)
            return carry

        return lax.fori_loop(0, pieces, piece, carry)

    lax.fori_loop(0, blocks, one_part, 0)
    lax.fori_loop(0, pieces, second, 0)
    lax.fori_loop(0, pieces, third, 0)
    lax.fori_loop(0, blocks, fourth, 0)

    dec_copy.wait_send()

    @pl.when(q < n_seq - 1)
    def _():
        for copy in halo_copies:
            copy.wait_send()

    def drain_state(c, carry):
        y_copy(c).wait_send()

        @pl.when(place < rows - 1)
        def _():
            z_copy(c).wait_send()

        return carry

    def drain_first(i, carry):
        near_copy(s1, r1, s1s, s1r, i).wait_send()
        far_copy(i).wait_send()
        return carry

    def drain_second(c, carry):
        near_copy(s3, r3, s3s, s3r, c).wait_send()
        return carry

    lax.fori_loop(0, chunks, drain_state, 0)
    lax.fori_loop(0, blocks * pieces, drain_first, 0)
    lax.fori_loop(0, pieces, drain_second, 0)


def on_device(n_seq, x_in, bc_in, z_in, dt_raw, a_log, conv_x, conv_bc, d_skip, norm_gain, out_weight):
    tokens, inner = x_in.shape
    heads = dt_raw.shape[0]
    features = out_weight.shape[1]
    state = bc_in.shape[2] // 2
    taps = conv_x.shape[0]
    blocks = tokens // SPAN
    chunks = inner // LANES
    per = heads // chunks
    share = features // 4
    cols = min(256, share)
    pieces = share // cols
    hbm = pl.BlockSpec(memory_space=pl.ANY)
    dma = pltpu.SemaphoreType.DMA
    vmem = pltpu.VMEM
    parts = vmem((blocks * pieces, SPAN, cols), BF16)
    wholes = vmem((pieces, tokens, cols), BF16)
    moved = vmem((chunks, state, LANES), BF16)
    return pl.pallas_call(
        functools.partial(layer_kernel, n_seq),
        name="layer",
        out_shape=jax.ShapeDtypeStruct((share, tokens), BF16),
        in_specs=[hbm] * 10,
        out_specs=pl.BlockSpec(memory_space=pltpu.VMEM),
        scratch_shapes=[
            vmem((tokens, inner), BF16),
            vmem((tokens, 2 * state), BF16),
            vmem((tokens, inner), BF16),
            vmem((heads, tokens), BF16),
            vmem((1, heads), F32),
            vmem((taps, inner), F32),
            vmem((1, taps * 2 * state), F32),
            vmem((1, heads), F32),
            vmem((1, inner), F32),
            vmem((4 * pieces, inner, cols), BF16),
            vmem((RIM, inner), BF16),
            vmem((RIM, 2 * state), BF16),
            vmem((tokens, inner), BF16),
            vmem((blocks, state, SPAN), BF16),
            vmem((blocks, SPAN, state), BF16),
            vmem((blocks, SPAN, SPAN), F32),
            vmem((blocks, chunks, per, SPAN), F32),
            vmem((blocks, chunks, per, SPAN), F32),
            vmem((blocks, chunks, SPAN, per), F32),
            vmem((blocks, SPAN, 2 * heads), BF16),
            vmem((blocks, SPAN, 2 * heads), BF16),
            vmem((2 * heads, inner), BF16),
            vmem((blocks, 8, inner), F32),
            vmem((blocks, 8, inner), F32),
            vmem((8, inner), F32),
            vmem((8, inner), F32),
            vmem((8, inner), F32),
            vmem((blocks, state, inner), F32),
            vmem((state, inner), F32),
            vmem((tokens, inner), F32),
            vmem((state, inner), F32),
            moved,
            moved,
            moved,
            moved,
            vmem((tokens, inner), BF16),
            parts,
            parts,
            parts,
            parts,
            wholes,
            wholes,
            vmem((pieces, tokens, cols), F32),
            dma((9,)),
            dma((4 * pieces,)),
            dma((4,)),
            dma((2,)),
            dma((chunks,)),
            dma((chunks,)),
            dma((chunks,)),
            dma((chunks,)),
            dma((blocks * pieces,)),
            dma((blocks * pieces,)),
            dma((blocks * pieces,)),
            dma((blocks * pieces,)),
            dma((pieces,)),
            dma((pieces,)),
        ],
        compiler_params=pltpu.CompilerParams(
            collective_id=0, has_side_effects=True, vmem_limit_bytes=60 * 2**20
        ),
    )(
        x_in,
        bc_in.reshape(tokens, 2 * state),
        z_in,
        dt_raw,
        a_log.reshape(1, heads),
        conv_x,
        conv_bc.reshape(1, taps * 2 * state),
        d_skip.reshape(1, heads),
        norm_gain.reshape(1, inner),
        out_weight,
    )


def solution(mesh):
    placed = (
        P("seq", "head"),
        P("seq", "head", None),
        P("seq", "head"),
        P("head", "seq"),
        P("head"),
        P(None, "head"),
        P(None, "head", None),
        P("head"),
        P("head"),
        P("head", None),
    )
    return jax.shard_map(
        functools.partial(on_device, mesh.shape["seq"]),
        mesh=mesh, in_specs=placed, out_specs=P("head", "seq"), check_vma=False,
    )
```

```python
import functools

import jax
import jax.numpy as jnp
from jax import lax
from jax.experimental import pallas as pl
from jax.experimental.pallas import tpu as pltpu
from jax.sharding import PartitionSpec as P

SPAN = 128
MESH = pl.DeviceIdType.MESH
F32 = jnp.float32
BF16 = jnp.bfloat16
LANES = 256
RIM = 16


def half_tanh_silu(u):
    return 0.5 * u * (1.0 + jnp.tanh(0.5 * u))


def conv_silu(before, now, taps):
    cat = jnp.concatenate([before.astype(F32), now.astype(F32)], 0)
    width = taps.shape[0]
    total = taps[width - 1 : width] * cat[RIM:]
    for k in range(width - 1):
        total = total + taps[k : k + 1] * pltpu.roll(cat, width - 1 - k, 0)[RIM:]
    return half_tanh_silu(total)


def layer_kernel(
    n_seq, x_hbm, bc_hbm, z_hbm, dt_hbm, alog_hbm, cx_hbm, cbc_hbm, skip_hbm, gain_hbm, w_hbm, out_ref,
    x_ref, bc_ref, z_ref, dt_ref, alog_ref, cx_ref, cbc_ref, skip_ref, gain_ref, w_buf,
    halo_x, halo_bc, xconv, b_t, b_mat, c_mat, score, ld_row, st_row, ld_col, t_tail, t_exp, pick,
    decay_in, decay_blk, decay_own, decay_other, skip_row, local_in, final, y_ref, enter,
    y_send, y_recv, z_send, z_recv, s1, r1, s2, r2, s3, r3, keep,
    in_sem, w_sem, halo_sems, dec_sems, ys_sem, yr_sem, zs_sem, zr_sem,
    s1s, s1r, s2s, s2r, s3s, s3r,
):
    tokens, inner = x_ref.shape
    heads = dt_ref.shape[0]
    state = b_t.shape[1]
    width = inner // heads
    blocks = tokens // SPAN
    chunks = inner // LANES
    per = heads // chunks
    rows = n_seq // 2
    pieces, cols = keep.shape[0], keep.shape[2]
    q = lax.axis_index("seq")
    odd = lax.rem(q, 2)
    place = q // 2
    pair = q + 1 - 2 * odd
    after = lax.rem(q + 1, n_seq)
    ahead = lax.rem(q + 2, n_seq)
    h = lax.axis_index("head")
    core = lax.rem(h, 2)
    side = h // 2
    near = 2 * side + 1 - core
    far = 2 * (1 - side) + core
    cross = 3 - h

    loads = [
        pltpu.make_async_copy(src, dst, in_sem.at[i])
        for i, (src, dst) in enumerate(
            [
                (dt_hbm, dt_ref), (alog_hbm, alog_ref), (skip_hbm, skip_ref), (bc_hbm, bc_ref), (cbc_hbm, cbc_ref),
                (cx_hbm, cx_ref), (x_hbm, x_ref), (gain_hbm, gain_ref), (z_hbm, z_ref),
            ]
        )
    ]
    for load in loads:
        load.start()

    barrier = pltpu.get_barrier_semaphore()
    pl.semaphore_signal(barrier, inc=1, device_id={"seq": pair}, device_id_type=MESH)
    for other in (near, far):
        pl.semaphore_signal(barrier, inc=1, device_id={"head": other}, device_id_type=MESH)

    @pl.when(q > 0)
    def _():
        pl.semaphore_signal(barrier, inc=1, device_id={"seq": q - 1}, device_id_type=MESH)

    @pl.when(q > 1)
    def _():
        pl.semaphore_signal(barrier, inc=1, device_id={"seq": q - 2}, device_id_type=MESH)

    def fetch(block, c, slot):
        start = pl.multiple_of((block * pieces + c) * cols, cols)
        return pltpu.make_async_copy(w_hbm.at[:, pl.ds(start, cols)], w_buf.at[slot], w_sem.at[slot])

    def fetch_all(act):
        def one(c, carry):
            act(fetch(cross, c, c))
            act(fetch(far, c, pieces + c))
            act(fetch(near, c, 2 * pieces + c))
            act(fetch(h, c, 3 * pieces + c))
            return carry

        lax.fori_loop(0, pieces, one, 0)

    peers = 3 + jnp.minimum(n_seq - 1 - q, 1) + jnp.minimum(jnp.maximum(n_seq - 2 - q, 0), 1)
    pl.semaphore_wait(barrier, peers)

    def send(src, dst, s, r, to):
        return pltpu.make_async_remote_copy(
            src_ref=src, dst_ref=dst, send_sem=s, recv_sem=r, device_id=to, device_id_type=MESH
        )

    halo_copies = [
        send(bc_hbm.at[pl.ds(tokens - RIM, RIM)], halo_bc, halo_sems.at[2], halo_sems.at[3], {"seq": after}),
        send(x_hbm.at[pl.ds(tokens - RIM, RIM)], halo_x, halo_sems.at[0], halo_sems.at[1], {"seq": after}),
    ]

    @pl.when(q < n_seq - 1)
    def _():
        for copy in halo_copies:
            copy.start()

    r_id = lax.broadcasted_iota(jnp.int32, (SPAN, SPAN), 0)
    c_id = lax.broadcasted_iota(jnp.int32, (SPAN, SPAN), 1)
    upto = jnp.where(r_id <= c_id, 1.0, 0.0).astype(F32)
    hr = lax.broadcasted_iota(jnp.int32, (heads, heads), 0)
    hc = lax.broadcasted_iota(jnp.int32, (heads, heads), 1)
    lane_head = lax.shift_right_logical(
        lax.broadcasted_iota(jnp.int32, (heads, inner), 1), jnp.full((heads, inner), width.bit_length() - 1, jnp.int32)
    )
    owner = lax.broadcasted_iota(jnp.int32, (heads, inner), 0) == lane_head
    ones = jnp.where(owner, 1.0, 0.0).astype(F32)
    pick[...] = jnp.concatenate([ones, ones], 0).astype(BF16)
    for load in loads[:3]:
        load.wait()
    neg_a = -jnp.sum(jnp.where(hr == hc, jnp.exp(alog_ref[...]), 0.0), axis=1, keepdims=True)
    dt = jnp.concatenate([dt_ref[:, b * SPAN : (b + 1) * SPAN].astype(F32) for b in range(blocks)], 0)
    e = jnp.exp(-jnp.abs(dt))
    log1p = jnp.where(e < 0.01, e * (1.0 - e * (0.5 - e * (1.0 / 3.0 - 0.25 * e))), jnp.log(1.0 + e))
    step = jnp.maximum(dt, 0.0) + log1p
    rate = jnp.concatenate([neg_a] * blocks, 0) * step
    ld = jnp.dot(rate, upto, preferred_element_type=F32, precision=lax.Precision.HIGHEST)
    tail = jnp.exp(ld[:, SPAN - 1 : SPAN] - ld) * step
    grow = jnp.exp(ld)

    def turned_pieces(value):
        high = value.astype(BF16).astype(F32)
        low = value - high
        parts = []
        for b in range(blocks):
            parts += [high[b * heads : (b + 1) * heads], low[b * heads : (b + 1) * heads]]
        turned = jnp.concatenate(parts, 0).T
        return [turned[:, 2 * heads * b : 2 * heads * (b + 1)].astype(BF16) for b in range(blocks)]

    tails = turned_pieces(tail)
    running = jnp.ones((8, inner), F32)
    for b in range(blocks):
        t_tail[b] = tails[b]
        last = jnp.sum(ones * grow[b * heads : (b + 1) * heads, SPAN - 1 : SPAN], axis=0, keepdims=True)
        decay_in[b] = running
        decay_blk[b] = jnp.broadcast_to(last, (8, inner))
        running = running * last
    decay_own[...] = running
    dec_copy = send(decay_own, decay_other, dec_sems.at[0], dec_sems.at[1], {"seq": pair})
    dec_copy.start()
    for load in loads[3:7]:
        load.wait()
    fetch_all(lambda copy: copy.start())

    @pl.when(q > 0)
    def _():
        for copy in halo_copies:
            copy.wait_recv()

    @pl.when(q == 0)
    def _():
        halo_x[...] = jnp.zeros_like(halo_x)
        halo_bc[...] = jnp.zeros_like(halo_bc)

    taps_bc = jnp.concatenate(
        [cbc_ref[:, k * 2 * state : (k + 1) * 2 * state] for k in range(cx_ref.shape[0])], 0
    )
    for b in range(blocks):
        before = halo_bc[...] if b == 0 else bc_ref[b * SPAN - RIM : b * SPAN]
        bc = conv_silu(before, bc_ref[b * SPAN : (b + 1) * SPAN], taps_bc)
        b_f = bc[:, :state].astype(BF16)
        c_f = bc[:, state:].astype(BF16)
        b_t[b] = bc[:, :state].T.astype(BF16)
        c_mat[b] = c_f
        b_mat[b] = b_f

    def y_copy(c):
        return send(y_send.at[c], y_recv.at[c], ys_sem.at[c], yr_sem.at[c], {"seq": pair})

    def z_copy(c):
        return send(z_send.at[c], z_recv.at[c], zs_sem.at[c], zr_sem.at[c], {"seq": ahead})

    mine_count = chunks // 2

    def state_chunk(j, carry):
        c = lax.rem((1 - odd) * mine_count + j, chunks)
        lanes = pl.ds(pl.multiple_of(c * LANES, LANES), LANES)
        held = jnp.zeros((state, LANES), F32)
        for b in range(blocks):
            tail = jnp.dot(t_tail[b], pick[:, lanes], preferred_element_type=F32)
            before = halo_x[:, lanes] if b == 0 else x_ref[pl.ds(b * SPAN - RIM, RIM), lanes]
            xc = conv_silu(before, x_ref[pl.ds(b * SPAN, SPAN), lanes], cx_ref[:, lanes]).astype(BF16)
            xconv[pl.ds(b * SPAN, SPAN), lanes] = xc
            weighted = (xc.astype(F32) * tail).astype(BF16)
            local_in[b, :, lanes] = held
            new = jnp.dot(b_t[b], weighted, preferred_element_type=F32)
            held = decay_blk[b, 0:1, lanes] * held + new
        final[:, lanes] = held

        @pl.when(j < mine_count)
        def _():
            y_send[c] = held.astype(BF16)
            y_copy(c).start()

        return carry

    lax.fori_loop(0, chunks, state_chunk, 0)

    skips = jnp.sum(jnp.where(hr == hc, jnp.broadcast_to(skip_ref[...], (heads, heads)), 0.0), axis=1, keepdims=True)
    skip_row[...] = jnp.broadcast_to(jnp.sum(ones * skips, axis=0, keepdims=True), (8, inner))
    grows, turned = turned_pieces(grow), ld.T
    for b in range(blocks):
        sc = lax.dot_general(c_mat[b], b_mat[b], (((1,), (1,)), ((), ())), preferred_element_type=F32)
        score[b] = jnp.where(r_id >= c_id, sc, 0.0)
        t_exp[b] = grows[b]
        for c in range(chunks):
            at = b * heads + c * per
            ld_row[b, c] = ld[at : at + per]
            st_row[b, c] = step[at : at + per]
            ld_col[b, c] = turned[:, at : at + per]
    dec_copy.wait_recv()
    is_odd = odd.astype(F32)

    def serve(m):
        c = odd * mine_count + m
        lanes = pl.ds(pl.multiple_of(c * LANES, LANES), LANES)
        y_copy(c).wait_recv()
        own = final[:, lanes]
        other = y_recv[c].astype(F32)
        d_own = decay_own[0:1, lanes]
        d_other = decay_other[0:1, lanes]
        y_send[c] = ((1.0 - is_odd) * own).astype(BF16)
        enter[:, lanes] = is_odd * other

        @pl.when(place < rows - 1)
        def _():
            final[:, lanes] = own * (is_odd + (1.0 - is_odd) * d_other) + other * (1.0 - is_odd + is_odd * d_own)

        @pl.when(place > 0)
        def _():
            z_copy(c).wait_recv()

            @pl.when(place < rows - 1)
            def _():
                final[:, lanes] += d_own * d_other * z_recv[c].astype(F32)

        @pl.when(place < rows - 1)
        def _():
            z_send[c] = final[:, lanes].astype(BF16)
            z_copy(c).start()

        @pl.when(place > 0)
        def _():
            before = z_recv[c].astype(F32)
            enter[:, lanes] += before * (1.0 - is_odd + is_odd * d_other)
            y_send[c] = ((1.0 - is_odd) * own + before * (is_odd + (1.0 - is_odd) * d_own)).astype(BF16)

        y_copy(c).start()

    def accept(m, carry):
        c = (1 - odd) * mine_count + m
        y_copy(c).wait_recv()
        enter[:, pl.ds(pl.multiple_of(c * LANES, LANES), LANES)] = y_recv[c].astype(F32)
        return carry

    first_head = lax.broadcasted_iota(jnp.int32, (1, 2 * width), 1) < width
    left = jnp.where(first_head, 1.0, 0.0).astype(BF16)
    right = jnp.where(first_head, 0.0, 1.0).astype(BF16)

    def intra(c):
        for b in range(blocks):
            token = pl.ds(b * SPAN, SPAN)
            lds = ld_row[b, c]
            sts = st_row[b, c]
            cl = ld_col[b, c]
            for j in range(per // 2):
                lanes = pl.ds(pl.multiple_of(c * LANES + j * 2 * width, 2 * width), 2 * width)
                mixes = []
                for i in (2 * j, 2 * j + 1):
                    gap = jnp.minimum(cl[:, i : i + 1] - lds[i : i + 1], 0.0)
                    mixes.append((score[b] * jnp.exp(gap) * sts[i : i + 1]).astype(BF16))
                xc = xconv[token, lanes]
                y_ref[token, lanes] = jnp.dot(
                    jnp.concatenate(mixes, 1),
                    jnp.concatenate([xc * left, xc * right], 0),
                    preferred_element_type=F32,
                )

    def slot(j, carry):
        m = j - 2 * place

        @pl.when((m >= 0) & (m < mine_count))
        def _():
            serve(m)

        @pl.when(j < chunks)
        def _():
            intra(j)

        return carry

    lax.fori_loop(0, max(chunks, mine_count + 2 * (rows - 1)), slot, 0)
    lax.fori_loop(0, mine_count, accept, 0)
    for load in loads[7:]:
        load.wait()
    fetch_all(lambda copy: copy.wait())

    def finish(b):
        token = pl.ds(pl.multiple_of(b * SPAN, SPAN), SPAN)
        power = jnp.zeros((SPAN, 1), F32)
        for c in range(chunks):
            lanes = pl.ds(c * LANES, LANES)
            grown = jnp.dot(t_exp[b], pick[:, lanes], preferred_element_type=F32)
            ent = (local_in[b, :, lanes] + decay_in[b, 0:1, lanes] * enter[:, lanes]).astype(BF16)
            read = jnp.dot(c_mat[b], ent, preferred_element_type=F32)
            total = y_ref[token, lanes] + grown * read + skip_row[0:1, lanes] * xconv[token, lanes].astype(F32)
            gated = total * half_tanh_silu(z_ref[token, lanes].astype(F32))
            y_ref[token, lanes] = gated
            power = power + jnp.sum(gated * gated, axis=1, keepdims=True)
        scale = lax.rsqrt(power * (1.0 / inner) + 1e-05)
        for c in range(chunks):
            lanes = pl.ds(c * LANES, LANES)
            x_ref[token, lanes] = (y_ref[token, lanes] * scale * gain_ref[:, lanes]).astype(BF16)

    def near_copy(src, dst, s, r, i):
        return send(src.at[i], dst.at[i], s.at[i], r.at[i], {"head": near})

    def far_copy(i):
        return send(s2.at[i], r2.at[i], s2s.at[i], s2r.at[i], {"head": far})

    def one_part(part, carry):
        token = pl.ds(pl.multiple_of(part * SPAN, SPAN), SPAN)
        finish(part)

        def pair_piece(c, carry):
            i = part * pieces + c
            s1[i] = jnp.dot(x_ref[token, :], w_buf[c], preferred_element_type=F32).astype(BF16)
            near_copy(s1, r1, s1s, s1r, i).start()
            return carry

        def far_piece(c, carry):
            i = part * pieces + c
            summed = jnp.dot(x_ref[token, :], w_buf[pieces + c], preferred_element_type=F32)
            near_copy(s1, r1, s1s, s1r, i).wait_recv()
            s2[i] = (summed + r1[i].astype(F32)).astype(BF16)
            far_copy(i).start()
            return carry

        lax.fori_loop(0, pieces, pair_piece, 0)
        lax.fori_loop(0, pieces, far_piece, 0)
        return carry

    def second(c, carry):
        s3[c] = jnp.dot(x_ref[...], w_buf[2 * pieces + c], preferred_element_type=F32).astype(BF16)
        near_copy(s3, r3, s3s, s3r, c).start()
        keep[c] = jnp.dot(x_ref[...], w_buf[3 * pieces + c], preferred_element_type=F32)
        return carry

    def third(c, carry):
        near_copy(s3, r3, s3s, s3r, c).wait_recv()
        keep[c] += r3[c].astype(F32)
        return carry

    def fourth(part, carry):
        token = pl.ds(pl.multiple_of(part * SPAN, SPAN), SPAN)

        def piece(c, carry):
            i = part * pieces + c
            far_copy(i).wait_recv()
            total = keep[c, token, :] + r2[i].astype(F32)
            out_ref[pl.ds(pl.multiple_of(c * cols, cols), cols), token] = total.T.astype(BF16)
            return carry

        return lax.fori_loop(0, pieces, piece, carry)

    lax.fori_loop(0, blocks, one_part, 0)
    lax.fori_loop(0, pieces, second, 0)
    lax.fori_loop(0, pieces, third, 0)
    lax.fori_loop(0, blocks, fourth, 0)

    dec_copy.wait_send()

    @pl.when(q < n_seq - 1)
    def _():
        for copy in halo_copies:
            copy.wait_send()

    def drain_state(c, carry):
        y_copy(c).wait_send()
        return carry

    def drain_chain(m, carry):
        @pl.when(place < rows - 1)
        def _():
            z_copy(odd * mine_count + m).wait_send()

        return carry

    def drain_first(i, carry):
        near_copy(s1, r1, s1s, s1r, i).wait_send()
        far_copy(i).wait_send()
        return carry

    def drain_second(c, carry):
        near_copy(s3, r3, s3s, s3r, c).wait_send()
        return carry

    lax.fori_loop(0, chunks, drain_state, 0)
    lax.fori_loop(0, mine_count, drain_chain, 0)
    lax.fori_loop(0, blocks * pieces, drain_first, 0)
    lax.fori_loop(0, pieces, drain_second, 0)


def on_device(n_seq, x_in, bc_in, z_in, dt_raw, a_log, conv_x, conv_bc, d_skip, norm_gain, out_weight):
    tokens, inner = x_in.shape
    heads = dt_raw.shape[0]
    features = out_weight.shape[1]
    state = bc_in.shape[2] // 2
    taps = conv_x.shape[0]
    blocks = tokens // SPAN
    chunks = inner // LANES
    per = heads // chunks
    share = features // 4
    cols = min(256, share)
    pieces = share // cols
    hbm = pl.BlockSpec(memory_space=pl.ANY)
    dma = pltpu.SemaphoreType.DMA
    vmem = pltpu.VMEM
    parts = vmem((blocks * pieces, SPAN, cols), BF16)
    wholes = vmem((pieces, tokens, cols), BF16)
    moved = vmem((chunks, state, LANES), BF16)
    return pl.pallas_call(
        functools.partial(layer_kernel, n_seq),
        name="layer",
        out_shape=jax.ShapeDtypeStruct((share, tokens), BF16),
        in_specs=[hbm] * 10,
        out_specs=pl.BlockSpec(memory_space=pltpu.VMEM),
        scratch_shapes=[
            vmem((tokens, inner), BF16),
            vmem((tokens, 2 * state), BF16),
            vmem((tokens, inner), BF16),
            vmem((heads, tokens), BF16),
            vmem((1, heads), F32),
            vmem((taps, inner), F32),
            vmem((1, taps * 2 * state), F32),
            vmem((1, heads), F32),
            vmem((1, inner), F32),
            vmem((4 * pieces, inner, cols), BF16),
            vmem((RIM, inner), BF16),
            vmem((RIM, 2 * state), BF16),
            vmem((tokens, inner), BF16),
            vmem((blocks, state, SPAN), BF16),
            vmem((blocks, SPAN, state), BF16),
            vmem((blocks, SPAN, state), BF16),
            vmem((blocks, SPAN, SPAN), F32),
            vmem((blocks, chunks, per, SPAN), F32),
            vmem((blocks, chunks, per, SPAN), F32),
            vmem((blocks, chunks, SPAN, per), F32),
            vmem((blocks, SPAN, 2 * heads), BF16),
            vmem((blocks, SPAN, 2 * heads), BF16),
            vmem((2 * heads, inner), BF16),
            vmem((blocks, 8, inner), F32),
            vmem((blocks, 8, inner), F32),
            vmem((8, inner), F32),
            vmem((8, inner), F32),
            vmem((8, inner), F32),
            vmem((blocks, state, inner), F32),
            vmem((state, inner), F32),
            vmem((tokens, inner), F32),
            vmem((state, inner), F32),
            moved,
            moved,
            moved,
            moved,
            parts,
            parts,
            parts,
            parts,
            wholes,
            wholes,
            vmem((pieces, tokens, cols), F32),
            dma((9,)),
            dma((4 * pieces,)),
            dma((4,)),
            dma((2,)),
            dma((chunks,)),
            dma((chunks,)),
            dma((chunks,)),
            dma((chunks,)),
            dma((blocks * pieces,)),
            dma((blocks * pieces,)),
            dma((blocks * pieces,)),
            dma((blocks * pieces,)),
            dma((pieces,)),
            dma((pieces,)),
        ],
        compiler_params=pltpu.CompilerParams(
            collective_id=0, has_side_effects=True, vmem_limit_bytes=60 * 2**20
        ),
    )(
        x_in,
        bc_in.reshape(tokens, 2 * state),
        z_in,
        dt_raw,
        a_log.reshape(1, heads),
        conv_x,
        conv_bc.reshape(1, taps * 2 * state),
        d_skip.reshape(1, heads),
        norm_gain.reshape(1, inner),
        out_weight,
    )


def solution(mesh):
    placed = (
        P("seq", "head"),
        P("seq", "head", None),
        P("seq", "head"),
        P("head", "seq"),
        P("head"),
        P(None, "head"),
        P(None, "head", None),
        P("head"),
        P("head"),
        P("head", None),
    )
    return jax.shard_map(
        functools.partial(on_device, mesh.shape["seq"]),
        mesh=mesh, in_specs=placed, out_specs=P("head", "seq"), check_vma=False,
    )
```
